32 devices in a mesh: seq: 16 (over z, y, core), head: 2 (over x).
Axes of the slice: x: 2, y: 2, z: 4, core: 2. Of those that a mesh axis runs over, the one named last changes fastest.
Arguments:
- prefix_embed: bfloat16 [256, 1024], replicated, may hold values from -6 to 6
- w_hidden: bfloat16 [1024, 8192], P(None, 'seq'), may hold values from -0.1875 to 0.1875
- b_hidden: float32 [8192], P('seq'), may hold values from -4 to 4
- w_out: bfloat16 [8192, 2, 1024], P('seq', None, 'head'), may hold values from -0.0625 to 0.0625
- queries: bfloat16 [2048, 8192], P('seq', 'head'), may hold values from -6 to 6
- keys: bfloat16 [2048, 1024], P('seq', 'head'), may hold values from -6 to 6
- values: bfloat16 [2048, 1024], P('seq', 'head'), may hold values from -6 to 6
- out_grad: bfloat16 [2048, 8192], P('seq', 'head'), may hold values from -6 to 6
Outputs:
- query_grad: bfloat16 [2048, 8192], P('seq', 'head')
- grad_w_out: float32 [8192, 2, 1024], P('seq', None, 'head')
- grad_w_hidden: float32 [1024, 8192], P(None, 'seq')
- grad_b_hidden: float32 [8192], P('seq')
- grad_prefix: float32 [256, 1024], replicated
The draws below stay inside these ranges and needn't reach their ends.
All inputs are finite; a program needn't handle non-finite values.
Results may differ from the reference program's by a relative error of at most 0.008.
Values may be sent and summed in bfloat16 or wider, within the bound.
A program may use at most 64 MiB of HBM per device.

```python
import math
import jax
import jax.numpy as jnp
from jax import lax

QH = 64
KVH = 8
HD = 128
NPRE = 256
EMB = 1024
HID = 8192
LENGTH = 2048
TOKENS = 2048
SEQS = 1
Q_W = 8192
KV_W = 1024


def draw_queries(key, part):
    total_rows = TOKENS
    base = jnp.clip(jax.random.normal(jax.random.fold_in(key, 11), (total_rows, QH * HD), jnp.float32), -6.0, 6.0)
    return base.astype(jnp.bfloat16)


def draw_keys(key, part):
    total_rows = TOKENS
    base = jnp.clip(jax.random.normal(jax.random.fold_in(key, 23), (total_rows, KVH * HD), jnp.float32), -6.0, 6.0)
    return base.astype(jnp.bfloat16)


def shard_levels(rng, dims, cuts, smallest, high):
    level = 1.0
    for position, shards_of in cuts:
        steps = jax.random.uniform(jax.random.fold_in(jax.random.fold_in(rng, 6), position), (shards_of,), jnp.float32, smallest / len(cuts), high / len(cuts))
        level = level * jnp.repeat(jnp.exp(steps), dims[position] // shards_of).reshape((-1,) + (1,) * (len(dims) - 1 - position))
    return level


def noise(stream_key, shape, width, most, cuts=(), held_as=jnp.bfloat16):
    loudness = shard_levels(stream_key, shape, cuts, -0.22, 0.18) if cuts else 1.0
    drawn = jax.random.normal(stream_key, shape, jnp.float32) * width * loudness
    return jnp.minimum(jnp.maximum(drawn, -most), most).astype(held_as)


def setup_inputs(seed: int = 0) -> dict:
    splits = jax.random.split(jax.random.key(seed), 9)
    prefix_embed = noise(splits[0], (NPRE, EMB), 1.0, 6.0)
    w_hidden = noise(splits[1], (EMB, HID), EMB ** -0.5, 0.1875, ((1, 16),))
    b_hidden = noise(splits[2], (HID,), 1.0, 4.0, ((0, 16),), jnp.float32)
    w_out = noise(splits[3], (HID, 2, KV_W), HID ** -0.5, 0.0625, ((0, 16), (2, 2)))
    queries = draw_queries(jax.random.fold_in(splits[8], 71), 0)
    keys = draw_keys(jax.random.fold_in(splits[8], 71), 0)
    values = noise(splits[6], (TOKENS, KV_W), 1.0, 6.0, ((0, 16), (1, 2)))
    out_grad = noise(splits[7], (TOKENS, Q_W), 1.0, 6.0, ((0, 16), (1, 2)))
    return dict(prefix_embed=prefix_embed, w_hidden=w_hidden, b_hidden=b_hidden, w_out=w_out, queries=queries, keys=keys, values=values, out_grad=out_grad)


def reference(prefix_embed, w_hidden, b_hidden, w_out, queries, keys, values, out_grad):
    scaling = 1.0 / math.sqrt(HD)
    group = QH // KVH
    hidden_pre = jnp.dot(prefix_embed, w_hidden, preferred_element_type=jnp.float32) + b_hidden
    tangent = jnp.tanh(hidden_pre)
    hidden = tangent.astype(jnp.bfloat16)
    prefix_kv = jnp.einsum('ph,hck->pck', hidden.astype(jnp.float32), w_out.astype(jnp.float32)).astype(jnp.bfloat16)
    prefix_keys = prefix_kv[:, 0]
    prefix_values = prefix_kv[:, 1]
    positions = jnp.arange(LENGTH, dtype=jnp.int32)
    causal = positions[None, :] <= positions[:, None]
    visible = jnp.concatenate([jnp.ones((LENGTH, NPRE), dtype=bool), causal], 1)

    def one_sequence(pieces):
        seq_queries, seq_keys, seq_values, seq_grads = pieces

        def one_head(head):
            kv_head = head // group
            query_rows = lax.dynamic_slice_in_dim(seq_queries, (head * HD).astype(jnp.int32), HD, 1)
            grad_rows = lax.dynamic_slice_in_dim(seq_grads, (head * HD).astype(jnp.int32), HD, 1)
            column = (kv_head * HD).astype(jnp.int32)
            key_all = jnp.concatenate([lax.dynamic_slice_in_dim(prefix_keys, column, HD, 1), lax.dynamic_slice_in_dim(seq_keys, column, HD, 1)], 0)
            value_all = jnp.concatenate([lax.dynamic_slice_in_dim(prefix_values, column, HD, 1), lax.dynamic_slice_in_dim(seq_values, column, HD, 1)], 0)
            logits = jnp.dot(query_rows, key_all.T, preferred_element_type=jnp.float32) * scaling
            logits = jnp.where(visible, logits, -jnp.inf)
            row_max = lax.optimization_barrier(jnp.max(logits, axis=1, keepdims=True))
            log_total = row_max + jnp.log(lax.optimization_barrier(jnp.sum(jnp.exp(logits - row_max), axis=1, keepdims=True)))
            probs = jnp.exp(logits - log_total)
            dot_grads = jnp.dot(grad_rows, value_all.T, preferred_element_type=jnp.float32)
            delta_row = lax.optimization_barrier(jnp.sum(probs * dot_grads, axis=1, keepdims=True))
            score_grad = (probs * (dot_grads - delta_row)).astype(jnp.bfloat16)
            probs_b = probs.astype(jnp.bfloat16)
            head_grad = (jnp.dot(score_grad, key_all, preferred_element_type=jnp.float32) * scaling).astype(jnp.bfloat16)
            key_grad = jnp.dot(score_grad[:, :NPRE].T, query_rows, preferred_element_type=jnp.float32) * scaling
            value_grad = jnp.dot(probs_b[:, :NPRE].T, grad_rows, preferred_element_type=jnp.float32)
            return (head_grad, key_grad, value_grad)
        head_grads, key_grads, value_grads = lax.map(one_head, jnp.arange(QH, dtype=jnp.int32))
        seq_query_grad = head_grads.transpose(1, 0, 2).reshape(LENGTH, QH * HD)
        key_sum = key_grads.reshape(KVH, group, NPRE, HD).sum(1).transpose(1, 0, 2).reshape(NPRE, KVH * HD)
        value_sum = value_grads.reshape(KVH, group, NPRE, HD).sum(1).transpose(1, 0, 2).reshape(NPRE, KVH * HD)
        return (seq_query_grad, key_sum, value_sum)
    stacked = (queries.reshape(SEQS, LENGTH, QH * HD), keys.reshape(SEQS, LENGTH, KVH * HD), values.reshape(SEQS, LENGTH, KVH * HD), out_grad.reshape(SEQS, LENGTH, QH * HD))
    seq_grads, key_sums, value_sums = lax.map(one_sequence, stacked)
    query_grad = seq_grads.reshape(SEQS * LENGTH, QH * HD)
    prefix_grads = jnp.stack([lax.optimization_barrier(jnp.sum(key_sums, axis=0)), lax.optimization_barrier(jnp.sum(value_sums, axis=0))], 1).astype(jnp.bfloat16)
    grad_w_out = jnp.einsum('ph,pck->hck', hidden.astype(jnp.float32), prefix_grads.astype(jnp.float32))
    hidden_grad = jnp.einsum('pck,hck->ph', prefix_grads.astype(jnp.float32), w_out.astype(jnp.float32))
    pre_grad = hidden_grad * (1.0 - tangent * tangent)
    pre_rounded = pre_grad.astype(jnp.bfloat16)
    grad_w_hidden = jnp.dot(prefix_embed.T, pre_rounded, preferred_element_type=jnp.float32)
    grad_b_hidden = lax.optimization_barrier(jnp.sum(pre_grad, axis=0))
    grad_prefix = jnp.dot(pre_rounded, w_hidden.T, preferred_element_type=jnp.float32)
    return (query_grad, grad_w_out, grad_w_hidden, grad_b_hidden, grad_prefix)
```

```python
import functools
import math

import jax
import jax.numpy as jnp
from jax import lax
from jax.experimental import pallas as pl
from jax.experimental.pallas import tpu as pltpu
from jax.sharding import PartitionSpec as P

QH = 64
KVH = 8
HD = 128
HEADS_PER_TILE = 4


def dot(a, b, dims):
    return lax.dot_general(a, b, (dims, ((), ())), preferred_element_type=jnp.float32)


NT = ((1,), (1,))
NN = ((1,), (0,))
TN = ((0,), (0,))


def fold_lanes(block, op):
    parts = [block[:, i : i + HD] for i in range(0, block.shape[1], HD)]
    return functools.reduce(op, parts)


def attention_kernel(
    pos_ref, q_ref, do_ref, k_ref, v_ref, pk_ref, pv_ref,
    dq_ref, kg_ref, vg_ref,
    q_s, do_s, s_s, d_s, ps_s, pd_s, m_s, l_s, dl_s, acc_s,
):
    tok = q_ref.shape[0]
    heads = q_ref.shape[1] // HD
    block = s_s.shape[2]
    scaling = 1.0 / math.sqrt(HD)
    to_exp2 = scaling * math.log2(math.e)
    my_start = pos_ref[0] * tok
    full = my_start // block

    for h in range(heads):
        q_s[h * tok : (h + 1) * tok, :] = q_ref[:, h * HD : (h + 1) * HD]
        do_s[h * tok : (h + 1) * tok, :] = do_ref[:, h * HD : (h + 1) * HD]

    s = dot(q_s[...], pk_ref[...], NT)
    ps_s[...] = s
    m_s[...] = fold_lanes(s, jnp.maximum)

    def logits(i):
        return dot(q_s[...], k_ref[pl.ds(pl.multiple_of(i * block, block), block), :], NT)

    def first(i, carry):
        s = logits(i)
        s_s[i] = s
        m_s[...] = jnp.maximum(m_s[...], fold_lanes(s, jnp.maximum))
        return carry

    lax.fori_loop(0, full, first, 0)
    s = logits(full)
    key_pos = full * block + lax.broadcasted_iota(jnp.int32, (tok, block), 1)
    query_pos = my_start + lax.broadcasted_iota(jnp.int32, (tok, block), 0)
    seen = key_pos <= query_pos
    s = jnp.where(seen[None], s.reshape(heads, tok, block), -1e30).reshape(s.shape)
    s_s[full] = s
    row_max = jnp.max(
        jnp.maximum(m_s[...], fold_lanes(s, jnp.maximum)), axis=1, keepdims=True
    )
    m_s[...] = jnp.broadcast_to(row_max, m_s.shape)

    p = jnp.exp2((ps_s[...] - m_s[:, :1]) * to_exp2)
    d = dot(do_s[...], pv_ref[...], NT)
    ps_s[...] = p
    pd_s[...] = d
    l_s[...] = fold_lanes(p, jnp.add)
    dl_s[...] = fold_lanes(p * d, jnp.add)

    def second(i, carry):
        d = dot(do_s[...], v_ref[pl.ds(pl.multiple_of(i * block, block), block), :], NT)
        p = jnp.exp2((s_s[i] - m_s[:, :1]) * to_exp2)
        s_s[i] = p
        d_s[i] = d
        l_s[...] += fold_lanes(p, jnp.add)
        dl_s[...] += fold_lanes(p * d, jnp.add)
        return carry

    lax.fori_loop(0, full + 1, second, 0)
    inverse = 1.0 / jnp.sum(l_s[...], axis=1, keepdims=True)
    delta = jnp.sum(dl_s[...], axis=1, keepdims=True) * inverse
    l_s[...] = jnp.broadcast_to(inverse, l_s.shape)
    dl_s[...] = jnp.broadcast_to(delta, dl_s.shape)
    acc_s[...] = jnp.zeros_like(acc_s)

    def third(i, carry):
        sg = (s_s[i] * (d_s[i] - dl_s[:, :1])).astype(jnp.bfloat16)
        acc_s[...] += dot(sg, k_ref[pl.ds(pl.multiple_of(i * block, block), block), :], NN)
        return carry

    lax.fori_loop(0, full + 1, third, 0)
    probs = ps_s[...] * l_s[:, :1]
    sg = (probs * (pd_s[...] - dl_s[:, :1])).astype(jnp.bfloat16)
    probs_b = probs.astype(jnp.bfloat16)
    dq = (acc_s[...] * l_s[...] + dot(sg, pk_ref[...], NN)) * scaling
    dq = dq.astype(jnp.bfloat16)
    for h in range(heads):
        dq_ref[:, h * HD : (h + 1) * HD] = dq[h * tok : (h + 1) * tok, :]
    kg = dot(sg, q_s[...], TN) * scaling
    vg = dot(probs_b, do_s[...], TN)

    @pl.when(pl.program_id(1) == 0)
    def _():
        kg_ref[...] = kg
        vg_ref[...] = vg

    @pl.when(pl.program_id(1) > 0)
    def _():
        kg_ref[...] += kg
        vg_ref[...] += vg


def attention(position, queries, out_grad, kv_all, prefix_kv):
    tok, q_width = queries.shape
    total, both = kv_all.shape
    heads_here = both // (2 * HD)
    group = QH // KVH
    per_tile = math.gcd(group, HEADS_PER_TILE)
    tiles = group // per_tile
    block = 2 * tok if total % (2 * tok) == 0 else tok
    rows = per_tile * tok
    prefix_len = prefix_kv.shape[0]
    row_block = pl.BlockSpec((tok, per_tile * HD), lambda g, j, pos: (0, g * tiles + j))
    key_block = pl.BlockSpec((total, HD), lambda g, j, pos: (0, g))
    value_block = pl.BlockSpec((total, HD), lambda g, j, pos: (0, heads_here + g))
    pk_block = pl.BlockSpec((prefix_len, HD), lambda g, j, pos: (0, g))
    pv_block = pl.BlockSpec((prefix_len, HD), lambda g, j, pos: (0, heads_here + g))
    f32 = jnp.float32
    return pl.pallas_call(
        attention_kernel,
        out_shape=(
            jax.ShapeDtypeStruct(queries.shape, jnp.bfloat16),
            jax.ShapeDtypeStruct((prefix_len, heads_here * HD), f32),
            jax.ShapeDtypeStruct((prefix_len, heads_here * HD), f32),
        ),
        grid_spec=pltpu.PrefetchScalarGridSpec(
            num_scalar_prefetch=1,
            grid=(heads_here, tiles),
            in_specs=[row_block, row_block, key_block, value_block, pk_block, pv_block],
            out_specs=(row_block, pk_block, pk_block),
            scratch_shapes=[
                pltpu.VMEM((rows, HD), jnp.bfloat16),
                pltpu.VMEM((rows, HD), jnp.bfloat16),
                pltpu.VMEM((total // block, rows, block), f32),
                pltpu.VMEM((total // block, rows, block), f32),
                pltpu.VMEM((rows, prefix_len), f32),
                pltpu.VMEM((rows, prefix_len), f32),
                pltpu.VMEM((rows, HD), f32),
                pltpu.VMEM((rows, HD), f32),
                pltpu.VMEM((rows, HD), f32),
                pltpu.VMEM((rows, HD), f32),
            ],
        ),
        compiler_params=pltpu.CompilerParams(vmem_limit_bytes=48 * 2**20),
    )(position, queries, out_grad, kv_all, kv_all, prefix_kv, prefix_kv)


def all_sum(value, axis):
    part = lax.psum_scatter(value, axis, scatter_dimension=0, tiled=True)
    return lax.all_gather(part.astype(jnp.bfloat16), axis, axis=0, tiled=True)


def on_device(prefix_embed, w_hidden, b_hidden, w_out, queries, keys, values, out_grad):
    columns = keys.shape[1]
    units = w_out.shape[0]
    kv_all = lax.all_gather(jnp.concatenate([keys, values], 1), "seq", axis=0, tiled=True)
    hidden_pre = jnp.dot(prefix_embed, w_hidden, preferred_element_type=jnp.float32) + b_hidden
    tangent = jnp.tanh(hidden_pre)
    hidden = tangent.astype(jnp.bfloat16)
    w_flat = w_out.reshape(units, 2 * columns)
    prefix_kv = all_sum(jnp.dot(hidden, w_flat, preferred_element_type=jnp.float32), "seq")
    position = lax.axis_index("seq").astype(jnp.int32).reshape(1)
    query_grad, key_grad, value_grad = attention(position, queries, out_grad, kv_all, prefix_kv)
    prefix_grads = all_sum(jnp.concatenate([key_grad, value_grad], 1), "seq")
    grad_w_out = dot(hidden, prefix_grads, TN).reshape(units, 2, columns)
    hidden_grad = lax.psum(dot(prefix_grads, w_flat, NT), "head")
    pre_grad = hidden_grad * (1.0 - tangent * tangent)
    pre_rounded = pre_grad.astype(jnp.bfloat16)
    grad_w_hidden = dot(prefix_embed, pre_rounded, TN)
    grad_b_hidden = jnp.sum(pre_grad, axis=0)
    grad_prefix = lax.psum(dot(pre_rounded, w_hidden, NT), "seq")
    return (query_grad, grad_w_out, grad_w_hidden, grad_b_hidden, grad_prefix)


def solution(mesh):
    placed = (
        P(),
        P(None, "seq"),
        P("seq"),
        P("seq", None, "head"),
        P("seq", "head"),
        P("seq", "head"),
        P("seq", "head"),
        P("seq", "head"),
    )
    return jax.shard_map(
        on_device,
        mesh=mesh,
        in_specs=placed,
        out_specs=(P("seq", "head"), P("seq", None, "head"), P(None, "seq"), P("seq"), P()),
        check_vma=False,
    )
```

```python
import functools
import math

import jax
import jax.numpy as jnp
from jax import lax
from jax.experimental import pallas as pl
from jax.experimental.pallas import tpu as pltpu
from jax.sharding import PartitionSpec as P

QH = 64
KVH = 8
HD = 128
HEADS_PER_TILE = 4


def dot(a, b, dims):
    return lax.dot_general(a, b, (dims, ((), ())), preferred_element_type=jnp.float32)


NT = ((1,), (1,))
NN = ((1,), (0,))
TN = ((0,), (0,))


def fold_lanes(block, op):
    parts = [block[:, i : i + HD] for i in range(0, block.shape[1], HD)]
    return functools.reduce(op, parts)


def attention_kernel(
    pos_ref, q_ref, do_ref, k_ref, v_ref, pk_ref, pv_ref,
    dq_ref, pg_ref,
    q_s, do_s, s_s, d_s, ps_s, pd_s, m_s, l_s, dl_s, acc_s,
):
    tok = q_ref.shape[0]
    heads = q_ref.shape[1] // HD
    block = s_s.shape[2]
    scaling = 1.0 / math.sqrt(HD)
    to_exp2 = scaling * math.log2(math.e)
    my_start = pos_ref[0] * tok
    full = my_start // block

    for h in range(heads):
        q_s[h * tok : (h + 1) * tok, :] = q_ref[:, h * HD : (h + 1) * HD]
        do_s[h * tok : (h + 1) * tok, :] = do_ref[:, h * HD : (h + 1) * HD]

    s = dot(q_s[...], pk_ref[...], NT)
    ps_s[...] = s
    m_s[...] = fold_lanes(s, jnp.maximum)

    def logits(i):
        return dot(q_s[...], k_ref[pl.ds(pl.multiple_of(i * block, block), block), :], NT)

    def first(i, carry):
        s = logits(i)
        s_s[i] = s
        m_s[...] = jnp.maximum(m_s[...], fold_lanes(s, jnp.maximum))
        return carry

    lax.fori_loop(0, full, first, 0)
    s = logits(full)
    key_pos = full * block + lax.broadcasted_iota(jnp.int32, (tok, block), 1)
    query_pos = my_start + lax.broadcasted_iota(jnp.int32, (tok, block), 0)
    seen = key_pos <= query_pos
    s = jnp.where(seen[None], s.reshape(heads, tok, block), -1e30).reshape(s.shape)
    s_s[full] = s
    row_max = jnp.max(
        jnp.maximum(m_s[...], fold_lanes(s, jnp.maximum)), axis=1, keepdims=True
    )
    m_s[...] = jnp.broadcast_to(row_max, m_s.shape)

    p = jnp.exp2((ps_s[...] - m_s[:, :1]) * to_exp2)
    d = dot(do_s[...], pv_ref[...], NT)
    ps_s[...] = p
    pd_s[...] = d
    l_s[...] = fold_lanes(p, jnp.add)
    dl_s[...] = fold_lanes(p * d, jnp.add)

    def second(i, carry):
        d = dot(do_s[...], v_ref[pl.ds(pl.multiple_of(i * block, block), block), :], NT)
        p = jnp.exp2((s_s[i] - m_s[:, :1]) * to_exp2)
        s_s[i] = p
        d_s[i] = d
        l_s[...] += fold_lanes(p, jnp.add)
        dl_s[...] += fold_lanes(p * d, jnp.add)
        return carry

    lax.fori_loop(0, full + 1, second, 0)
    inverse = 1.0 / jnp.sum(l_s[...], axis=1, keepdims=True)
    delta = jnp.sum(dl_s[...], axis=1, keepdims=True) * inverse
    l_s[...] = jnp.broadcast_to(inverse, l_s.shape)
    dl_s[...] = jnp.broadcast_to(delta, dl_s.shape)
    acc_s[...] = jnp.zeros_like(acc_s)

    def third(i, carry):
        sg = (s_s[i] * (d_s[i] - dl_s[:, :1])).astype(jnp.bfloat16)
        acc_s[...] += dot(sg, k_ref[pl.ds(pl.multiple_of(i * block, block), block), :], NN)
        return carry

    lax.fori_loop(0, full + 1, third, 0)
    probs = ps_s[...] * l_s[:, :1]
    sg = (probs * (pd_s[...] - dl_s[:, :1])).astype(jnp.bfloat16)
    probs_b = probs.astype(jnp.bfloat16)
    dq = (acc_s[...] * l_s[...] + dot(sg, pk_ref[...], NN)) * scaling
    dq = dq.astype(jnp.bfloat16)
    for h in range(heads):
        dq_ref[:, h * HD : (h + 1) * HD] = dq[h * tok : (h + 1) * tok, :]
    kg = dot(sg, q_s[...], TN) * scaling
    vg = dot(probs_b, do_s[...], TN)

    @pl.when(pl.program_id(1) == 0)
    def _():
        pg_ref[0] = kg
        pg_ref[1] = vg

    @pl.when(pl.program_id(1) > 0)
    def _():
        pg_ref[0] += kg
        pg_ref[1] += vg


def attention(position, queries, out_grad, kv_all, prefix_kv):
    tok, q_width = queries.shape
    total, both = kv_all.shape
    heads_here = both // (2 * HD)
    group = QH // KVH
    per_tile = math.gcd(group, HEADS_PER_TILE)
    tiles = group // per_tile
    block = 2 * tok if total % (2 * tok) == 0 else tok
    rows = per_tile * tok
    prefix_len = prefix_kv.shape[0] // 2
    row_block = pl.BlockSpec((tok, per_tile * HD), lambda g, j, pos: (0, g * tiles + j))
    key_block = pl.BlockSpec((total, HD), lambda g, j, pos: (0, g))
    value_block = pl.BlockSpec((total, HD), lambda g, j, pos: (0, heads_here + g))
    pk_block = pl.BlockSpec((prefix_len, HD), lambda g, j, pos: (0, g))
    pv_block = pl.BlockSpec((prefix_len, HD), lambda g, j, pos: (1, g))
    pg_block = pl.BlockSpec((2, prefix_len, HD), lambda g, j, pos: (0, 0, g))
    f32 = jnp.float32
    return pl.pallas_call(
        attention_kernel,
        out_shape=(
            jax.ShapeDtypeStruct(queries.shape, jnp.bfloat16),
            jax.ShapeDtypeStruct((2, prefix_len, heads_here * HD), f32),
        ),
        grid_spec=pltpu.PrefetchScalarGridSpec(
            num_scalar_prefetch=1,
            grid=(heads_here, tiles),
            in_specs=[row_block, row_block, key_block, value_block, pk_block, pv_block],
            out_specs=(row_block, pg_block),
            scratch_shapes=[
                pltpu.VMEM((rows, HD), jnp.bfloat16),
                pltpu.VMEM((rows, HD), jnp.bfloat16),
                pltpu.VMEM((total // block, rows, block), f32),
                pltpu.VMEM((total // block, rows, block), f32),
                pltpu.VMEM((rows, prefix_len), f32),
                pltpu.VMEM((rows, prefix_len), f32),
                pltpu.VMEM((rows, HD), f32),
                pltpu.VMEM((rows, HD), f32),
                pltpu.VMEM((rows, HD), f32),
                pltpu.VMEM((rows, HD), f32),
            ],
        ),
        compiler_params=pltpu.CompilerParams(vmem_limit_bytes=48 * 2**20),
    )(position, queries, out_grad, kv_all, kv_all, prefix_kv, prefix_kv)


MESH = pl.DeviceIdType.MESH


def sum_kernel(levels, paired, x_ref, o_ref, *scratch):
    recv, held = scratch[:levels], scratch[levels : 2 * levels]
    send_sem, recv_sem = scratch[2 * levels :]
    me = lax.axis_index("seq")
    bits = [(me // 2**k) % 2 for k in range(levels)]
    partners = [me + 2**k * (1 - 2 * bits[k]) for k in range(levels)]
    barrier = pltpu.get_barrier_semaphore()
    for partner in partners:
        pl.semaphore_signal(barrier, inc=1, device_id={"seq": partner}, device_id_type=MESH)
    if paired:
        head = lax.axis_index("head")
        other = 1 - head
        pl.semaphore_signal(barrier, inc=1, device_id={"head": other}, device_id_type=MESH)
    pl.semaphore_wait(barrier, levels + (1 if paired else 0))

    rows = x_ref.shape[0]
    source = x_ref
    copies = []
    starts = []
    start = 0
    for k in range(levels):
        half = rows // 2 ** (k + 1)
        copy = pltpu.make_async_remote_copy(
            src_ref=source.at[pl.ds(pl.multiple_of((1 - bits[k]) * half, half), half)],
            dst_ref=recv[k],
            send_sem=send_sem.at[k],
            recv_sem=recv_sem.at[k],
            device_id={"seq": partners[k]},
            device_id_type=MESH,
        )
        copy.start()
        copy.wait_recv()
        held[k][...] = source[pl.ds(pl.multiple_of(bits[k] * half, half), half), :] + recv[k][...]
        source = held[k]
        copies.append(copy)
        start = start + bits[k] * half
        starts.append(start)
    out = o_ref.at[head] if paired else o_ref.at[0]
    last = rows // 2**levels
    out[pl.ds(pl.multiple_of(start, last), last), :] = source[...].astype(o_ref.dtype)
    for k in reversed(range(levels)):
        half = rows // 2 ** (k + 1)
        part = out.at[pl.ds(pl.multiple_of(starts[k], half), half)]
        copy = pltpu.make_async_remote_copy(
            src_ref=part,
            dst_ref=part,
            send_sem=send_sem.at[levels + k],
            recv_sem=recv_sem.at[levels + k],
            device_id={"seq": partners[k]},
            device_id_type=MESH,
        )
        copy.start()
        copy.wait_recv()
        copies.append(copy)
    if paired:
        copy = pltpu.make_async_remote_copy(
            src_ref=out,
            dst_ref=out,
            send_sem=send_sem.at[2 * levels],
            recv_sem=recv_sem.at[2 * levels],
            device_id={"head": other},
            device_id_type=MESH,
        )
        copy.start()
        copy.wait_recv()
        copies.append(copy)
    for copy in copies:
        copy.wait_send()


def all_sum(value, collective_id, paired=False):
    rows, columns = value.shape
    levels = lax.axis_size("seq").bit_length() - 1
    shapes = [pltpu.VMEM((rows // 2 ** (k + 1), columns), jnp.float32) for k in range(levels)]
    return pl.pallas_call(
        functools.partial(sum_kernel, levels, paired),
        out_shape=jax.ShapeDtypeStruct((2 if paired else 1, rows, columns), jnp.bfloat16),
        in_specs=[pl.BlockSpec(memory_space=pltpu.VMEM)],
        out_specs=pl.BlockSpec(memory_space=pltpu.VMEM),
        scratch_shapes=shapes
        + shapes
        + [
            pltpu.SemaphoreType.DMA((2 * levels + 1,)),
            pltpu.SemaphoreType.DMA((2 * levels + 1,)),
        ],
        compiler_params=pltpu.CompilerParams(
            collective_id=collective_id, has_side_effects=True, vmem_limit_bytes=24 * 2**20
        ),
    )(value)


def on_device(prefix_embed, w_hidden, b_hidden, w_out, queries, keys, values, out_grad):
    columns = keys.shape[1]
    emb = w_hidden.shape[0]
    prefix_len = prefix_embed.shape[0]
    kv_all = lax.all_gather(jnp.concatenate([keys, values], 1), "seq", axis=0, tiled=True)
    hidden_pre = jnp.dot(prefix_embed, w_hidden, preferred_element_type=jnp.float32) + b_hidden
    tangent = jnp.tanh(hidden_pre)
    hidden = tangent.astype(jnp.bfloat16)
    w_key, w_value = w_out[:, 0], w_out[:, 1]
    partial_kv = jnp.concatenate([dot(hidden, w_key, NN), dot(hidden, w_value, NN)], 0)
    prefix_kv = all_sum(partial_kv, 0)[0]
    position = lax.axis_index("seq").astype(jnp.int32).reshape(1)
    query_grad, both_grads = attention(position, queries, out_grad, kv_all, prefix_kv)
    prefix_grads = all_sum(both_grads.reshape(2 * prefix_len, columns), 1)[0]
    pg_key, pg_value = prefix_grads[:prefix_len], prefix_grads[prefix_len:]
    hidden_part = dot(pg_key, w_key, NT) + dot(pg_value, w_value, NT)
    if lax.axis_size("head") == 2:
        hidden_grad = hidden_part + lax.ppermute(hidden_part, "head", [(0, 1), (1, 0)])
    else:
        hidden_grad = lax.psum(hidden_part, "head")
    grad_w_out = jnp.stack([dot(hidden, pg_key, TN), dot(hidden, pg_value, TN)], 1)
    pre_grad = hidden_grad * (1.0 - tangent * tangent)
    pre_rounded = pre_grad.astype(jnp.bfloat16)
    paired = lax.axis_size("head") == 2 and emb % 512 == 0
    share = emb // 2 if paired else emb
    if paired:
        w_share = lax.dynamic_slice_in_dim(w_hidden, lax.axis_index("head") * share, share, 0)
    else:
        w_share = w_hidden
    low = dot(pre_rounded, w_share[: share // 2], NT)
    high = dot(pre_rounded, w_share[share // 2 :], NT)
    summed = all_sum(jnp.concatenate([low, high], 0), 2, paired)
    grad_w_hidden = dot(prefix_embed, pre_rounded, TN)
    grad_b_hidden = jnp.sum(pre_grad, axis=0)
    summed = summed.reshape(-1, prefix_len, share // 2)
    grad_prefix = jnp.concatenate([summed[i] for i in range(summed.shape[0])], 1)
    grad_prefix = grad_prefix.astype(jnp.float32)
    return (query_grad, grad_w_out, grad_w_hidden, grad_b_hidden, grad_prefix)


def solution(mesh):
    placed = (
        P(),
        P(None, "seq"),
        P("seq"),
        P("seq", None, "head"),
        P("seq", "head"),
        P("seq", "head"),
        P("seq", "head"),
        P("seq", "head"),
    )
    return jax.shard_map(
        on_device,
        mesh=mesh,
        in_specs=placed,
        out_specs=(P("seq", "head"), P("seq", None, "head"), P(None, "seq"), P("seq"), P()),
        check_vma=False,
    )
```

```python
import functools
import math

import jax
import jax.numpy as jnp
from jax import lax
from jax.experimental import pallas as pl
from jax.experimental.pallas import tpu as pltpu
from jax.sharding import PartitionSpec as P

QH = 64
KVH = 8
HD = 128
HEADS_PER_TILE = 8


def dot(a, b, dims):
    return lax.dot_general(a, b, (dims, ((), ())), preferred_element_type=jnp.float32)


NT = ((1,), (1,))
NN = ((1,), (0,))
TN = ((0,), (0,))


def fold_lanes(block, op):
    parts = [block[:, i : i + HD] for i in range(0, block.shape[1], HD)]
    return functools.reduce(op, parts)


def widen(rows, width):
    return jnp.concatenate([rows] * (width // HD), axis=1)


def attention_kernel(
    pos_ref, q_ref, do_ref, k_ref, v_ref, pk_ref, pv_ref,
    dq_ref, pg_ref,
    q_s, do_s, s_s, d_s, ps_s, pd_s, m_s, l_s, dl_s, acc_s,
):
    tok = q_ref.shape[0]
    heads = q_ref.shape[1] // HD
    block = s_s.shape[2]
    scaling = 1.0 / math.sqrt(HD)
    to_exp2 = scaling * math.log2(math.e)
    my_start = pos_ref[0] * tok
    full = my_start // block

    for h in range(heads):
        q_s[h * tok : (h + 1) * tok, :] = q_ref[:, h * HD : (h + 1) * HD]
        do_s[h * tok : (h + 1) * tok, :] = do_ref[:, h * HD : (h + 1) * HD]

    s = dot(q_s[...], pk_ref[...], NT)
    ps_s[...] = s
    m_s[...] = fold_lanes(s, jnp.maximum)

    def logits(i):
        return dot(q_s[...], k_ref[pl.ds(pl.multiple_of(i * block, block), block), :], NT)

    def first(i, carry):
        s = logits(i)
        s_s[i] = s
        m_s[...] = jnp.maximum(m_s[...], fold_lanes(s, jnp.maximum))
        return carry

    lax.fori_loop(0, full, first, 0)
    s = logits(full)
    key_pos = full * block + lax.broadcasted_iota(jnp.int32, (tok, block), 1)
    query_pos = my_start + lax.broadcasted_iota(jnp.int32, (tok, block), 0)
    seen = key_pos <= query_pos
    s = jnp.where(seen[None], s.reshape(heads, tok, block), -1e30).reshape(s.shape)
    s_s[full] = s
    row_max = jnp.max(
        jnp.maximum(m_s[...], fold_lanes(s, jnp.maximum)), axis=1, keepdims=True
    )
    m_s[...] = jnp.broadcast_to(row_max, m_s.shape)

    p = jnp.exp2((ps_s[...] - widen(m_s[...], ps_s.shape[1])) * to_exp2)
    d = dot(do_s[...], pv_ref[...], NT)
    ps_s[...] = p
    pd_s[...] = d
    l_s[...] = fold_lanes(p, jnp.add)
    dl_s[...] = fold_lanes(p * d, jnp.add)

    def second(i, carry):
        d = dot(do_s[...], v_ref[pl.ds(pl.multiple_of(i * block, block), block), :], NT)
        p = jnp.exp2((s_s[i] - widen(m_s[...], block)) * to_exp2)
        s_s[i] = p
        d_s[i] = d
        l_s[...] += fold_lanes(p, jnp.add)
        dl_s[...] += fold_lanes(p * d, jnp.add)
        return carry

    lax.fori_loop(0, full + 1, second, 0)
    inverse = 1.0 / jnp.sum(l_s[...], axis=1, keepdims=True)
    delta = jnp.sum(dl_s[...], axis=1, keepdims=True) * inverse
    l_s[...] = jnp.broadcast_to(inverse, l_s.shape)
    dl_s[...] = jnp.broadcast_to(delta, dl_s.shape)
    acc_s[...] = jnp.zeros_like(acc_s)

    def third(i, carry):
        sg = (s_s[i] * (d_s[i] - widen(dl_s[...], block))).astype(jnp.bfloat16)
        acc_s[...] += dot(sg, k_ref[pl.ds(pl.multiple_of(i * block, block), block), :], NN)
        return carry

    lax.fori_loop(0, full + 1, third, 0)
    probs = ps_s[...] * widen(l_s[...], ps_s.shape[1])
    sg = (probs * (pd_s[...] - widen(dl_s[...], pd_s.shape[1]))).astype(jnp.bfloat16)
    probs_b = probs.astype(jnp.bfloat16)
    dq = (acc_s[...] * l_s[...] + dot(sg, pk_ref[...], NN)) * scaling
    dq = dq.astype(jnp.bfloat16)
    for h in range(heads):
        dq_ref[:, h * HD : (h + 1) * HD] = dq[h * tok : (h + 1) * tok, :]
    kg = dot(sg, q_s[...], TN) * scaling
    vg = dot(probs_b, do_s[...], TN)

    @pl.when(pl.program_id(1) == 0)
    def _():
        pg_ref[0] = kg
        pg_ref[1] = vg

    @pl.when(pl.program_id(1) > 0)
    def _():
        pg_ref[0] += kg
        pg_ref[1] += vg


def attention(position, queries, out_grad, kv_all, prefix_kv):
    tok, q_width = queries.shape
    total, both = kv_all.shape
    heads_here = both // (2 * HD)
    group = QH // KVH
    per_tile = math.gcd(group, HEADS_PER_TILE)
    tiles = group // per_tile
    block = 2 * tok if total % (2 * tok) == 0 else tok
    rows = per_tile * tok
    prefix_len = prefix_kv.shape[0] // 2
    row_block = pl.BlockSpec((tok, per_tile * HD), lambda g, j, pos: (0, g * tiles + j))
    key_block = pl.BlockSpec((total, HD), lambda g, j, pos: (0, g))
    value_block = pl.BlockSpec((total, HD), lambda g, j, pos: (0, heads_here + g))
    pk_block = pl.BlockSpec((prefix_len, HD), lambda g, j, pos: (0, g))
    pv_block = pl.BlockSpec((prefix_len, HD), lambda g, j, pos: (1, g))
    pg_block = pl.BlockSpec((2, prefix_len, HD), lambda g, j, pos: (0, 0, g))
    f32 = jnp.float32
    return pl.pallas_call(
        attention_kernel,
        out_shape=(
            jax.ShapeDtypeStruct(queries.shape, jnp.bfloat16),
            jax.ShapeDtypeStruct((2, prefix_len, heads_here * HD), f32),
        ),
        grid_spec=pltpu.PrefetchScalarGridSpec(
            num_scalar_prefetch=1,
            grid=(heads_here, tiles),
            in_specs=[row_block, row_block, key_block, value_block, pk_block, pv_block],
            out_specs=(row_block, pg_block),
            scratch_shapes=[
                pltpu.VMEM((rows, HD), jnp.bfloat16),
                pltpu.VMEM((rows, HD), jnp.bfloat16),
                pltpu.VMEM((total // block, rows, block), f32),
                pltpu.VMEM((total // block, rows, block), f32),
                pltpu.VMEM((rows, prefix_len), f32),
                pltpu.VMEM((rows, prefix_len), f32),
                pltpu.VMEM((rows, HD), f32),
                pltpu.VMEM((rows, HD), f32),
                pltpu.VMEM((rows, HD), f32),
                pltpu.VMEM((rows, HD), f32),
            ],
        ),
        compiler_params=pltpu.CompilerParams(vmem_limit_bytes=48 * 2**20),
    )(position, queries, out_grad, kv_all, kv_all, prefix_kv, prefix_kv)


MESH = pl.DeviceIdType.MESH


def sum_kernel(levels, orders, paired, x_ref, o_ref, *scratch):
    chunks = range(len(orders))
    recv = [scratch[c * levels : (c + 1) * levels] for c in chunks]
    scratch = scratch[len(orders) * levels :]
    held = [scratch[c * levels : (c + 1) * levels] for c in chunks]
    send_sem, recv_sem = scratch[len(orders) * levels :]
    me = lax.axis_index("seq")
    bits = [(me // 2**k) % 2 for k in range(levels)]
    partners = [me + 2**k * (1 - 2 * bits[k]) for k in range(levels)]
    barrier = pltpu.get_barrier_semaphore()
    for partner in partners:
        pl.semaphore_signal(barrier, inc=1, device_id={"seq": partner}, device_id_type=MESH)
    if paired:
        head = lax.axis_index("head")
        other = 1 - head
        pl.semaphore_signal(barrier, inc=1, device_id={"head": other}, device_id_type=MESH)
    pl.semaphore_wait(barrier, levels + (1 if paired else 0))

    rows = x_ref.shape[0]
    width = x_ref.shape[1] // len(orders)
    out = o_ref.at[head] if paired else o_ref.at[0]
    source = [x_ref.at[:, pl.ds(c * width, width)] for c in chunks]
    copies = []
    starts = [[] for c in chunks]
    start = [0 for c in chunks]
    for step in range(levels):
        half = rows // 2 ** (step + 1)
        going = []
        for c in chunks:
            k = orders[c][step]
            copy = pltpu.make_async_remote_copy(
                src_ref=source[c].at[pl.ds(pl.multiple_of((1 - bits[k]) * half, half), half)],
                dst_ref=recv[c][step],
                send_sem=send_sem.at[c, step],
                recv_sem=recv_sem.at[c, step],
                device_id={"seq": partners[k]},
                device_id_type=MESH,
            )
            copy.start()
            going.append(copy)
        for c in chunks:
            k = orders[c][step]
            going[c].wait_recv()
            kept = source[c][pl.ds(pl.multiple_of(bits[k] * half, half), half), :]
            held[c][step][...] = kept + recv[c][step][...]
            source[c] = held[c][step]
            start[c] = start[c] + bits[k] * half
            starts[c].append(start[c])
        copies += going
    last = rows // 2**levels
    for c in chunks:
        out[pl.ds(pl.multiple_of(start[c], last), last), pl.ds(c * width, width)] = source[c][
            ...
        ].astype(o_ref.dtype)
    for step in reversed(range(levels)):
        half = rows // 2 ** (step + 1)
        going = []
        for c in chunks:
            part = out.at[
                pl.ds(pl.multiple_of(starts[c][step], half), half), pl.ds(c * width, width)
            ]
            copy = pltpu.make_async_remote_copy(
                src_ref=part,
                dst_ref=part,
                send_sem=send_sem.at[c, levels + step],
                recv_sem=recv_sem.at[c, levels + step],
                device_id={"seq": partners[orders[c][step]]},
                device_id_type=MESH,
            )
            copy.start()
            going.append(copy)
        for copy in going:
            copy.wait_recv()
        copies += going
    if paired:
        copy = pltpu.make_async_remote_copy(
            src_ref=out,
            dst_ref=out,
            send_sem=send_sem.at[0, 2 * levels],
            recv_sem=recv_sem.at[0, 2 * levels],
            device_id={"head": other},
            device_id_type=MESH,
        )
        copy.start()
        copy.wait_recv()
        copies.append(copy)
    for copy in copies:
        copy.wait_send()


def all_sum(value, collective_id, paired=False):
    rows, columns = value.shape
    levels = lax.axis_size("seq").bit_length() - 1
    orders = [list(range(levels))]
    if columns % (2 * HD) == 0 and levels > 2:
        orders.append([0] + list(range(2, levels)) + [1])
    width = columns // len(orders)
    shapes = [pltpu.VMEM((rows // 2 ** (k + 1), width), jnp.float32) for k in range(levels)]
    return pl.pallas_call(
        functools.partial(sum_kernel, levels, orders, paired),
        out_shape=jax.ShapeDtypeStruct((2 if paired else 1, rows, columns), jnp.bfloat16),
        in_specs=[pl.BlockSpec(memory_space=pltpu.VMEM)],
        out_specs=pl.BlockSpec(memory_space=pltpu.VMEM),
        scratch_shapes=shapes * (2 * len(orders))
        + [
            pltpu.SemaphoreType.DMA((len(orders), 2 * levels + 1)),
            pltpu.SemaphoreType.DMA((len(orders), 2 * levels + 1)),
        ],
        compiler_params=pltpu.CompilerParams(
            collective_id=collective_id, has_side_effects=True, vmem_limit_bytes=24 * 2**20
        ),
    )(value)


def on_device(prefix_embed, w_hidden, b_hidden, w_out, queries, keys, values, out_grad):
    columns = keys.shape[1]
    emb = w_hidden.shape[0]
    prefix_len = prefix_embed.shape[0]
    kv_all = lax.all_gather(jnp.concatenate([keys, values], 1), "seq", axis=0, tiled=True)
    hidden_pre = jnp.dot(prefix_embed, w_hidden, preferred_element_type=jnp.float32) + b_hidden
    tangent = jnp.tanh(hidden_pre)
    hidden = tangent.astype(jnp.bfloat16)
    w_key, w_value = w_out[:, 0], w_out[:, 1]
    partial_kv = jnp.concatenate([dot(hidden, w_key, NN), dot(hidden, w_value, NN)], 0)
    prefix_kv = all_sum(partial_kv, 0)[0]
    position = lax.axis_index("seq").astype(jnp.int32).reshape(1)
    query_grad, both_grads = attention(position, queries, out_grad, kv_all, prefix_kv)
    prefix_grads = all_sum(both_grads.reshape(2 * prefix_len, columns), 1)[0]
    pg_key, pg_value = prefix_grads[:prefix_len], prefix_grads[prefix_len:]
    hidden_part = dot(pg_key, w_key, NT) + dot(pg_value, w_value, NT)
    if lax.axis_size("head") == 2:
        mine = hidden_part.astype(jnp.bfloat16)
        theirs = lax.ppermute(mine, "head", [(0, 1), (1, 0)])
        hidden_grad = mine.astype(jnp.float32) + theirs.astype(jnp.float32)
    else:
        hidden_grad = lax.psum(hidden_part, "head")
    grad_w_out = jnp.stack([dot(hidden, pg_key, TN), dot(hidden, pg_value, TN)], 1)
    pre_grad = hidden_grad * (1.0 - tangent * tangent)
    pre_rounded = pre_grad.astype(jnp.bfloat16)
    paired = lax.axis_size("head") == 2 and emb % 512 == 0
    share = emb // 2 if paired else emb
    if paired:
        w_share = lax.dynamic_slice_in_dim(w_hidden, lax.axis_index("head") * share, share, 0)
    else:
        w_share = w_hidden
    low = dot(pre_rounded, w_share[: share // 2], NT)
    high = dot(pre_rounded, w_share[share // 2 :], NT)
    summed = all_sum(jnp.concatenate([low, high], 0), 2, paired)
    grad_w_hidden = dot(prefix_embed, pre_rounded, TN)
    grad_b_hidden = jnp.sum(pre_grad, axis=0)
    summed = summed.reshape(-1, prefix_len, share // 2)
    grad_prefix = jnp.concatenate([summed[i] for i in range(summed.shape[0])], 1)
    grad_prefix = grad_prefix.astype(jnp.float32)
    return (query_grad, grad_w_out, grad_w_hidden, grad_b_hidden, grad_prefix)


def solution(mesh):
    placed = (
        P(),
        P(None, "seq"),
        P("seq"),
        P("seq", None, "head"),
        P("seq", "head"),
        P("seq", "head"),
        P("seq", "head"),
        P("seq", "head"),
    )
    return jax.shard_map(
        on_device,
        mesh=mesh,
        in_specs=placed,
        out_specs=(P("seq", "head"), P("seq", None, "head"), P(None, "seq"), P("seq"), P()),
        check_vma=False,
    )
```

```python
import functools
import math

import jax
import jax.numpy as jnp
from jax import lax
from jax.experimental import pallas as pl
from jax.experimental.pallas import tpu as pltpu
from jax.sharding import PartitionSpec as P

QH = 64
KVH = 8
HD = 128
HEADS_PER_TILE = 8


def dot(a, b, dims):
    return lax.dot_general(a, b, (dims, ((), ())), preferred_element_type=jnp.float32)


NT = ((1,), (1,))
NN = ((1,), (0,))
TN = ((0,), (0,))


def fold_lanes(block, op):
    parts = [block[:, i : i + HD] for i in range(0, block.shape[1], HD)]
    return functools.reduce(op, parts)


def widen(rows, width):
    return jnp.concatenate([rows] * (width // HD), axis=1)


def attention_kernel(
    pos_ref, q_ref, do_ref, k_ref, v_ref, pk_ref, pv_ref,
    dq_ref, pg_ref,
    q_s, do_s, s_s, d_s, ps_s, pd_s, m_s, l_s, dl_s, acc_s,
):
    tok = q_ref.shape[0]
    heads = q_ref.shape[1] // HD
    block = s_s.shape[2]
    scaling = 1.0 / math.sqrt(HD)
    to_exp2 = scaling * math.log2(math.e)
    my_start = pos_ref[0] * tok
    full = my_start // block

    for h in range(heads):
        q_s[h * tok : (h + 1) * tok, :] = q_ref[:, h * HD : (h + 1) * HD]
        do_s[h * tok : (h + 1) * tok, :] = do_ref[:, h * HD : (h + 1) * HD]

    s = dot(q_s[...], pk_ref[...], NT)
    ps_s[...] = s
    m_s[...] = fold_lanes(s, jnp.maximum)

    def logits(i):
        return dot(q_s[...], k_ref[pl.ds(pl.multiple_of(i * block, block), block), :], NT)

    def first(i, carry):
        s = logits(i)
        s_s[i] = s
        m_s[...] = jnp.maximum(m_s[...], fold_lanes(s, jnp.maximum))
        return carry

    lax.fori_loop(0, full, first, 0)
    s = logits(full)
    key_pos = full * block + lax.broadcasted_iota(jnp.int32, (tok, block), 1)
    query_pos = my_start + lax.broadcasted_iota(jnp.int32, (tok, block), 0)
    seen = key_pos <= query_pos
    s = jnp.where(seen[None], s.reshape(heads, tok, block), -1e30).reshape(s.shape)
    s_s[full] = s
    row_max = jnp.max(
        jnp.maximum(m_s[...], fold_lanes(s, jnp.maximum)), axis=1, keepdims=True
    )
    m_s[...] = jnp.broadcast_to(row_max, m_s.shape)

    p = jnp.exp2((ps_s[...] - widen(m_s[...], ps_s.shape[1])) * to_exp2)
    d = dot(do_s[...], pv_ref[...], NT)
    ps_s[...] = p
    pd_s[...] = d
    l_s[...] = fold_lanes(p, jnp.add)
    dl_s[...] = fold_lanes(p * d, jnp.add)

    def second(i, carry):
        d = dot(do_s[...], v_ref[pl.ds(pl.multiple_of(i * block, block), block), :], NT)
        p = jnp.exp2((s_s[i] - widen(m_s[...], block)) * to_exp2)
        s_s[i] = p
        d_s[i] = d
        l_s[...] += fold_lanes(p, jnp.add)
        dl_s[...] += fold_lanes(p * d, jnp.add)
        return carry

    lax.fori_loop(0, full + 1, second, 0)
    inverse = 1.0 / jnp.sum(l_s[...], axis=1, keepdims=True)
    delta = jnp.sum(dl_s[...], axis=1, keepdims=True) * inverse
    l_s[...] = jnp.broadcast_to(inverse, l_s.shape)
    dl_s[...] = jnp.broadcast_to(delta, dl_s.shape)
    acc_s[...] = jnp.zeros_like(acc_s)

    def third(i, carry):
        sg = (s_s[i] * (d_s[i] - widen(dl_s[...], block))).astype(jnp.bfloat16)
        acc_s[...] += dot(sg, k_ref[pl.ds(pl.multiple_of(i * block, block), block), :], NN)
        return carry

    lax.fori_loop(0, full + 1, third, 0)
    probs = ps_s[...] * widen(l_s[...], ps_s.shape[1])
    sg = (probs * (pd_s[...] - widen(dl_s[...], pd_s.shape[1]))).astype(jnp.bfloat16)
    probs_b = probs.astype(jnp.bfloat16)
    dq = (acc_s[...] * l_s[...] + dot(sg, pk_ref[...], NN)) * scaling
    dq = dq.astype(jnp.bfloat16)
    for h in range(heads):
        dq_ref[:, h * HD : (h + 1) * HD] = dq[h * tok : (h + 1) * tok, :]
    kg = dot(sg, q_s[...], TN) * scaling
    vg = dot(probs_b, do_s[...], TN)

    @pl.when(pl.program_id(1) == 0)
    def _():
        pg_ref[0] = kg
        pg_ref[1] = vg

    @pl.when(pl.program_id(1) > 0)
    def _():
        pg_ref[0] += kg
        pg_ref[1] += vg


def attention(position, queries, out_grad, kv_all, prefix_kv):
    tok, q_width = queries.shape
    total, both = kv_all.shape
    heads_here = both // (2 * HD)
    group = QH // KVH
    per_tile = math.gcd(group, HEADS_PER_TILE)
    tiles = group // per_tile
    block = next(n * tok for n in (4, 2, 1) if total % (n * tok) == 0)
    rows = per_tile * tok
    prefix_len = prefix_kv.shape[0] // 2
    row_block = pl.BlockSpec((tok, per_tile * HD), lambda g, j, pos: (0, g * tiles + j))
    key_block = pl.BlockSpec((total, HD), lambda g, j, pos: (0, g))
    value_block = pl.BlockSpec((total, HD), lambda g, j, pos: (0, heads_here + g))
    pk_block = pl.BlockSpec((prefix_len, HD), lambda g, j, pos: (0, g))
    pv_block = pl.BlockSpec((prefix_len, HD), lambda g, j, pos: (1, g))
    pg_block = pl.BlockSpec((2, prefix_len, HD), lambda g, j, pos: (0, 0, g))
    f32 = jnp.float32
    return pl.pallas_call(
        attention_kernel,
        out_shape=(
            jax.ShapeDtypeStruct(queries.shape, jnp.bfloat16),
            jax.ShapeDtypeStruct((2, prefix_len, heads_here * HD), f32),
        ),
        grid_spec=pltpu.PrefetchScalarGridSpec(
            num_scalar_prefetch=1,
            grid=(heads_here, tiles),
            in_specs=[row_block, row_block, key_block, value_block, pk_block, pv_block],
            out_specs=(row_block, pg_block),
            scratch_shapes=[
                pltpu.VMEM((rows, HD), jnp.bfloat16),
                pltpu.VMEM((rows, HD), jnp.bfloat16),
                pltpu.VMEM((total // block, rows, block), f32),
                pltpu.VMEM((total // block, rows, block), f32),
                pltpu.VMEM((rows, prefix_len), f32),
                pltpu.VMEM((rows, prefix_len), f32),
                pltpu.VMEM((rows, HD), f32),
                pltpu.VMEM((rows, HD), f32),
                pltpu.VMEM((rows, HD), f32),
                pltpu.VMEM((rows, HD), f32),
            ],
        ),
        compiler_params=pltpu.CompilerParams(vmem_limit_bytes=48 * 2**20),
    )(position, queries, out_grad, kv_all, kv_all, prefix_kv, prefix_kv)


MESH = pl.DeviceIdType.MESH


def sum_kernel(levels, orders, paired, x_ref, o_ref, *scratch):
    chunks = range(len(orders))
    recv = [scratch[c * levels : (c + 1) * levels] for c in chunks]
    scratch = scratch[len(orders) * levels :]
    held = [scratch[c * levels : (c + 1) * levels] for c in chunks]
    send_sem, recv_sem = scratch[len(orders) * levels :]
    me = lax.axis_index("seq")
    bits = [(me // 2**k) % 2 for k in range(levels)]
    partners = [me + 2**k * (1 - 2 * bits[k]) for k in range(levels)]
    barrier = pltpu.get_barrier_semaphore()
    for partner in partners:
        pl.semaphore_signal(barrier, inc=1, device_id={"seq": partner}, device_id_type=MESH)
    if paired:
        head = lax.axis_index("head")
        other = 1 - head
        pl.semaphore_signal(barrier, inc=1, device_id={"head": other}, device_id_type=MESH)
    pl.semaphore_wait(barrier, levels + (1 if paired else 0))

    rows = x_ref.shape[0]
    width = x_ref.shape[1] // len(orders)
    out = o_ref.at[head] if paired else o_ref.at[0]
    source = [x_ref.at[:, pl.ds(c * width, width)] for c in chunks]
    copies = []
    starts = [[] for c in chunks]
    start = [0 for c in chunks]
    for step in range(levels):
        half = rows // 2 ** (step + 1)
        going = []
        for c in chunks:
            k = orders[c][step]
            copy = pltpu.make_async_remote_copy(
                src_ref=source[c].at[pl.ds(pl.multiple_of((1 - bits[k]) * half, half), half)],
                dst_ref=recv[c][step],
                send_sem=send_sem.at[c, step],
                recv_sem=recv_sem.at[c, step],
                device_id={"seq": partners[k]},
                device_id_type=MESH,
            )
            copy.start()
            going.append(copy)
        for c in chunks:
            k = orders[c][step]
            going[c].wait_recv()
            kept = source[c][pl.ds(pl.multiple_of(bits[k] * half, half), half), :]
            held[c][step][...] = kept + recv[c][step][...]
            source[c] = held[c][step]
            start[c] = start[c] + bits[k] * half
            starts[c].append(start[c])
        copies += going
    last = rows // 2**levels
    for c in chunks:
        out[pl.ds(pl.multiple_of(start[c], last), last), pl.ds(c * width, width)] = source[c][
            ...
        ].astype(o_ref.dtype)
    for step in reversed(range(levels)):
        half = rows // 2 ** (step + 1)
        going = []
        for c in chunks:
            part = out.at[
                pl.ds(pl.multiple_of(starts[c][step], half), half), pl.ds(c * width, width)
            ]
            copy = pltpu.make_async_remote_copy(
                src_ref=part,
                dst_ref=part,
                send_sem=send_sem.at[c, levels + step],
                recv_sem=recv_sem.at[c, levels + step],
                device_id={"seq": partners[orders[c][step]]},
                device_id_type=MESH,
            )
            copy.start()
            going.append(copy)
        for copy in going:
            copy.wait_recv()
        copies += going
    if paired:
        copy = pltpu.make_async_remote_copy(
            src_ref=out,
            dst_ref=out,
            send_sem=send_sem.at[0, 2 * levels],
            recv_sem=recv_sem.at[0, 2 * levels],
            device_id={"head": other},
            device_id_type=MESH,
        )
        copy.start()
        copy.wait_recv()
        copies.append(copy)
    for copy in copies:
        copy.wait_send()


def all_sum(value, collective_id, paired=False):
    rows, columns = value.shape
    levels = lax.axis_size("seq").bit_length() - 1
    orders = [list(range(levels))]
    if columns % (2 * HD) == 0 and levels > 2:
        orders.append([0] + list(range(2, levels)) + [1])
    width = columns // len(orders)
    shapes = [pltpu.VMEM((rows // 2 ** (k + 1), width), jnp.float32) for k in range(levels)]
    return pl.pallas_call(
        functools.partial(sum_kernel, levels, orders, paired),
        out_shape=jax.ShapeDtypeStruct((2 if paired else 1, rows, columns), jnp.bfloat16),
        in_specs=[pl.BlockSpec(memory_space=pltpu.VMEM)],
        out_specs=pl.BlockSpec(memory_space=pltpu.VMEM),
        scratch_shapes=shapes * (2 * len(orders))
        + [
            pltpu.SemaphoreType.DMA((len(orders), 2 * levels + 1)),
            pltpu.SemaphoreType.DMA((len(orders), 2 * levels + 1)),
        ],
        compiler_params=pltpu.CompilerParams(
            collective_id=collective_id, has_side_effects=True, vmem_limit_bytes=24 * 2**20
        ),
    )(value)


def on_device(prefix_embed, w_hidden, b_hidden, w_out, queries, keys, values, out_grad):
    columns = keys.shape[1]
    emb = w_hidden.shape[0]
    prefix_len = prefix_embed.shape[0]
    kv_all = lax.all_gather(jnp.concatenate([keys, values], 1), "seq", axis=0, tiled=True)
    hidden_pre = jnp.dot(prefix_embed, w_hidden, preferred_element_type=jnp.float32) + b_hidden
    tangent = jnp.tanh(hidden_pre)
    hidden = tangent.astype(jnp.bfloat16)
    w_key, w_value = w_out[:, 0], w_out[:, 1]
    partial_kv = jnp.concatenate([dot(hidden, w_key, NN), dot(hidden, w_value, NN)], 0)
    prefix_kv = all_sum(partial_kv, 0)[0]
    position = lax.axis_index("seq").astype(jnp.int32).reshape(1)
    query_grad, both_grads = attention(position, queries, out_grad, kv_all, prefix_kv)
    prefix_grads = all_sum(both_grads.reshape(2 * prefix_len, columns), 1)[0]
    pg_key, pg_value = prefix_grads[:prefix_len], prefix_grads[prefix_len:]
    hidden_part = dot(pg_key, w_key, NT) + dot(pg_value, w_value, NT)
    if lax.axis_size("head") == 2:
        mine = hidden_part.astype(jnp.bfloat16)
        theirs = lax.ppermute(mine, "head", [(0, 1), (1, 0)])
        hidden_grad = mine.astype(jnp.float32) + theirs.astype(jnp.float32)
    else:
        hidden_grad = lax.psum(hidden_part, "head")
    grad_w_out = jnp.stack([dot(hidden, pg_key, TN), dot(hidden, pg_value, TN)], 1)
    pre_grad = hidden_grad * (1.0 - tangent * tangent)
    pre_rounded = pre_grad.astype(jnp.bfloat16)
    paired = lax.axis_size("head") == 2 and emb % 512 == 0
    share = emb // 2 if paired else emb
    if paired:
        w_share = lax.dynamic_slice_in_dim(w_hidden, lax.axis_index("head") * share, share, 0)
    else:
        w_share = w_hidden
    low = dot(pre_rounded, w_share[: share // 2], NT)
    high = dot(pre_rounded, w_share[share // 2 :], NT)
    summed = all_sum(jnp.concatenate([low, high], 0), 2, paired)
    grad_w_hidden = dot(prefix_embed, pre_rounded, TN)
    grad_b_hidden = jnp.sum(pre_grad, axis=0)
    summed = summed.reshape(-1, prefix_len, share // 2)
    grad_prefix = jnp.concatenate([summed[i] for i in range(summed.shape[0])], 1)
    grad_prefix = grad_prefix.astype(jnp.float32)
    return (query_grad, grad_w_out, grad_w_hidden, grad_b_hidden, grad_prefix)


def solution(mesh):
    placed = (
        P(),
        P(None, "seq"),
        P("seq"),
        P("seq", None, "head"),
        P("seq", "head"),
        P("seq", "head"),
        P("seq", "head"),
        P("seq", "head"),
    )
    return jax.shard_map(
        on_device,
        mesh=mesh,
        in_specs=placed,
        out_specs=(P("seq", "head"), P("seq", None, "head"), P(None, "seq"), P("seq"), P()),
        check_vma=False,
    )
```
